512 devices in a mesh: section: 2 (over core), dp: 32 (over x_lo, z), tensor: 8 (over y, x_hi).
Axes of the slice: x: 4 (x_hi: 2, x_lo: 2; x = x_hi * 2 + x_lo), y: 4, z: 16, core: 2. Of those that a mesh axis runs over, the one named last changes fastest.
Arguments:
- projections: bfloat16 [2, 3, 8192, 6144], P('section', None, 'dp', 'tensor'), may hold values from -5 to 5
- out_grad: bfloat16 [8192, 6144], P('dp', 'tensor'), may hold values from -6 to 6
Outputs:
- grads: bfloat16 [2, 3, 8192, 6144], P('section', None, 'dp', 'tensor')
The draws below stay inside these ranges and needn't reach their ends.
All inputs are finite; a program needn't handle non-finite values.
Results may differ from the reference program's by a relative error of at most 0.01.
Values may be sent and summed in bfloat16 or wider, within the bound.
No kernel may reach another device: no remote copies, remote signals or barrier semaphores. Data moves between devices by JAX's collectives and lax.ppermute only.
A program may use at most 128 MiB of HBM per device.

```python
import math
import jax
import jax.numpy as jnp
from jax import lax

HEADS = 48
HD = 128
TOK_DEV = 256
LEN = 1024
SEQS = 8
TOKENS = 8192
N_DP = 32
N_TENSOR = 8


def stored_order(logical):
    parts = logical.reshape(N_DP, 2, TOK_DEV // 2, N_TENSOR // 2, 2 * HEADS * HD // N_TENSOR).transpose(0, 3, 1, 2, 4)
    parts = parts.reshape(N_DP, N_TENSOR, TOK_DEV, HEADS * HD // N_TENSOR)
    return parts.transpose(0, 2, 1, 3).reshape(TOKENS, HEADS * HD)


def draw_projections(key, part):
    key = jax.random.fold_in(key, 11)
    base_key = jax.random.fold_in(key, 0)
    shape = (2, 3, TOKENS, HEADS * HD)
    whole = jnp.clip(jax.random.normal(base_key, shape, jnp.float32), -5.0, 5.0)
    later = jnp.stack([stored_order(whole[1, 0]), stored_order(whole[1, 1]), stored_order(whole[1, 2])])
    return jnp.stack([whole[0], later]).astype(jnp.bfloat16)


def block_scale(key, dims, cuts, smallest, high):
    def one(dim, blocks):
        heights = jax.random.uniform(jax.random.fold_in(jax.random.fold_in(key, 6), dim), (blocks,), jnp.float32, smallest / len(cuts), high / len(cuts))
        return jnp.repeat(jnp.exp(heights), dims[dim] // blocks).reshape((-1,) + (1,) * (len(dims) - dim - 1))

    gain = one(*cuts[0])
    for cut in cuts[1:]:
        gain = gain * one(*cut)
    return gain


def gaussian(rng, shape, width, most, cuts=(), dtype=jnp.bfloat16):
    level = block_scale(rng, shape, cuts, -0.22, 0.18) if cuts else 1.0
    entries = jax.random.normal(rng, shape, jnp.float32) * width * level
    return jnp.minimum(jnp.maximum(entries, -most), most).astype(dtype)


def setup_inputs(seed: int = 0) -> dict:
    streams_of = jax.random.split(jax.random.key(seed), 3)
    projections = draw_projections(jax.random.fold_in(streams_of[2], 71), 0)
    out_grad = gaussian(streams_of[1], (TOKENS, HEADS * HD), 1.0, 6.0, ((0, 32), (1, 8)))
    return {"projections": projections, "out_grad": out_grad}


def unstore(stored):
    parts = stored.reshape(N_DP, TOK_DEV, N_TENSOR, HEADS * HD // N_TENSOR).transpose(0, 2, 1, 3)
    parts = parts.reshape(N_DP, N_TENSOR // 2, 2, TOK_DEV // 2, 2 * HEADS * HD // N_TENSOR)
    return parts.transpose(0, 2, 3, 1, 4).reshape(TOKENS, HEADS * HD)

def restore(logical):
    parts = logical.reshape(N_DP, 2, TOK_DEV // 2, N_TENSOR // 2, 2 * HEADS * HD // N_TENSOR).transpose(0, 3, 1, 2, 4)
    parts = parts.reshape(N_DP, N_TENSOR, TOK_DEV, HEADS * HD // N_TENSOR)
    return parts.transpose(0, 2, 1, 3).reshape(TOKENS, HEADS * HD)

def to_heads(matrix):
    return matrix.reshape(SEQS, LEN, HEADS, HD).transpose(0, 2, 1, 3).reshape(SEQS * HEADS, LEN, HD)

def from_heads(stacked):
    return stacked.reshape(SEQS, HEADS, LEN, HD).transpose(0, 2, 1, 3).reshape(SEQS * LEN, HEADS * HD)

def head_scores(query, keys):
    scores = jnp.dot(query, keys.T, preferred_element_type=jnp.float32) * (1.0 / math.sqrt(HD))
    row_pos = lax.broadcasted_iota(jnp.int32, (LEN, LEN), 0)
    col_pos = lax.broadcasted_iota(jnp.int32, (LEN, LEN), 1)
    return jnp.where(col_pos <= row_pos, scores, -jnp.inf)

def forward(queries, keys, values):

    def single(item):
        query, key_rows, value_rows = item
        scores = head_scores(query, key_rows)
        top = lax.optimization_barrier(jnp.max(scores, axis=1, keepdims=True))
        lse = top + jnp.log(lax.optimization_barrier(jnp.sum(jnp.exp(scores - top), axis=1, keepdims=True)))
        probs = jnp.exp(scores - lse).astype(jnp.bfloat16)
        out = jnp.dot(probs, value_rows, preferred_element_type=jnp.float32).astype(jnp.bfloat16)
        return (out, lse)
    out, lse = lax.map(single, (to_heads(queries), to_heads(keys), to_heads(values)))
    return (from_heads(out), lse)

def block_terms(left, right, factor, block_len):
    blocks = LEN // block_len
    left_blocks = left.astype(jnp.float32).reshape(blocks, block_len, LEN)
    right_blocks = right.astype(jnp.float32).reshape(blocks, block_len, HD)
    terms = jnp.einsum('gqk,gqd->gkd', left_blocks, right_blocks, precision=lax.Precision.HIGHEST) * factor
    rounded = lax.optimization_barrier(terms.astype(jnp.bfloat16))
    return lax.optimization_barrier(jnp.sum(rounded.astype(jnp.float32), axis=0)).astype(jnp.bfloat16)

def backward(queries, keys, values, outputs, lse, cotangent, block_len):
    scale = 1.0 / math.sqrt(HD)

    def single(item):
        query, key_rows, value_rows, out, lse_rows, grad = item
        probs = jnp.exp(head_scores(query, key_rows) - lse_rows)
        delta = lax.optimization_barrier(jnp.sum(grad.astype(jnp.float32) * out.astype(jnp.float32), axis=1, keepdims=True))
        dvals = block_terms(probs.astype(jnp.bfloat16), grad, 1.0, block_len)
        dprobs = jnp.dot(grad, value_rows.T, preferred_element_type=jnp.float32)
        dscore = (probs * (dprobs - delta)).astype(jnp.bfloat16)
        dquery = jnp.dot(dscore, key_rows, preferred_element_type=jnp.float32) * scale
        dkeys = block_terms(dscore, query, scale, block_len)
        return (dquery.astype(jnp.bfloat16), dkeys, dvals)
    dquery, dkeys, dvals = lax.map(single, (to_heads(queries), to_heads(keys), to_heads(values), to_heads(outputs), lse, to_heads(cotangent)))
    return (from_heads(dquery), from_heads(dkeys), from_heads(dvals))

def reference(projections, out_grad):
    first_q, first_k, first_v = (projections[0, 0], projections[0, 1], projections[0, 2])
    first_out, first_lse = forward(first_q, first_k, first_v)
    second_q = (unstore(projections[1, 0]).astype(jnp.float32) + first_out.astype(jnp.float32)).astype(jnp.bfloat16)
    second_k, second_v = (unstore(projections[1, 1]), unstore(projections[1, 2]))
    second_out, second_lse = forward(second_q, second_k, second_v)
    dq_two, dk_two, dv_two = backward(second_q, second_k, second_v, second_out, second_lse, unstore(out_grad), TOK_DEV // 2)
    dq_one, dk_one, dv_one = backward(first_q, first_k, first_v, first_out, first_lse, dq_two, TOK_DEV)
    second = jnp.stack([restore(dq_two), restore(dk_two), restore(dv_two)])
    return jnp.stack([jnp.stack([dq_one, dk_one, dv_one]), second])
```

```python
import math

import jax
import jax.numpy as jnp
from jax import lax
from jax.experimental import pallas as pl
from jax.experimental.pallas import tpu as pltpu
from jax.sharding import PartitionSpec as P

HD = 128
BLK = 256
LEN = 1024
SCALE = 1.0 / math.sqrt(HD)
SCALE2 = SCALE * math.log2(math.e)
AXES = ("section", "dp", "tensor")
BF = jnp.bfloat16
F32 = jnp.float32
VM = pl.BlockSpec(memory_space=pltpu.VMEM)
SM = pl.BlockSpec(memory_space=pltpu.SMEM)


def first_head(z):
    return jnp.where(z > 0, z + 1, 0)


def second_head(z):
    return jnp.where(z == 3, 5, 1)


def is_edge(z):
    return (z == 0) | (z == 3)


def head_cols(head):
    return pl.ds(pl.multiple_of(head * HD, HD), HD)


def rows_of(index, size):
    return pl.ds(pl.multiple_of(index * size, size), size)


def dot(a, b):
    return jnp.dot(a, b, preferred_element_type=F32)


def flip(x):
    return x.astype(F32).T.astype(BF)


def call(kernel, outs, args, scratch=(), flops=0):
    return pl.pallas_call(
        kernel,
        out_shape=[jax.ShapeDtypeStruct(s, d) for s, d in outs],
        in_specs=[SM] + [VM] * (len(args) - 1),
        out_specs=[VM] * len(outs),
        scratch_shapes=list(scratch),
        compiler_params=pltpu.CompilerParams(vmem_limit_bytes=48 * 1024 * 1024),
        cost_estimate=pl.CostEstimate(flops=flops, bytes_accessed=4000000, transcendentals=0),
    )(*args)


def pick_kernel(info, local, grad, *outs):
    z, h = info[0], info[1]
    for k in range(4):
        other = z ^ k
        outs[k][...] = local[:, :, head_cols(first_head(other))]
        outs[4 + k][...] = local[:, :, head_cols(second_head(other))]
    own, away = outs[8], outs[9]
    row = lax.broadcasted_iota(jnp.int32, (128, 256), 0)
    col = lax.broadcasted_iota(jnp.int32, (128, 256), 1)
    for out, a in ((own, h), (away, 1 - h)):
        take = jnp.where(col == 2 * row + a, 1.0, 0.0).astype(BF)
        for j in range(4):
            rows = grad[...] if j == 3 else local[j]
            out[j] = dot(take, rows).astype(BF)


def pick_second_kernel(info, own, came, *outs):
    z, h = info[0], info[1]
    mine, theirs = rows_of(h, 128), rows_of(1 - h, 128)
    for k in range(4):
        for slot, head in ((0, first_head(z ^ k)), (4, second_head(z ^ k))):
            outs[slot + k][:, mine, :] = own[:, :, head_cols(head)]
            outs[slot + k][:, theirs, :] = came[:, :, head_cols(head)]


def assemble(info, slot_a, slot_b, dst):
    z, s = info[0], info[2]

    @pl.when(s == 0)
    def _():
        for k in range(4):
            dst[:, rows_of(z ^ k, BLK), :] = slot_a[k][...]

    @pl.when(s == 1)
    def _():
        for k in range(4):
            dst[:, rows_of(z ^ k, BLK), :] = slot_b[k][...]


def score_block(keys, qt, i):
    n = (i + 1) * BLK
    st = dot(keys[0:n], qt[:, i * BLK : n]) * SCALE2
    key = lax.broadcasted_iota(jnp.int32, (BLK, BLK), 0)
    qry = lax.broadcasted_iota(jnp.int32, (BLK, BLK), 1)
    tail = jnp.where(key <= qry, st[n - BLK :], -jnp.inf)
    return tail if i == 0 else jnp.concatenate([st[: n - BLK], tail], axis=0)


def forward_kernel(info, *refs):
    slot_a, slot_b = refs[0:4], refs[4:8]
    qkv, ot, lse = refs[8:11]
    qt, vt = refs[11:]
    assemble(info, slot_a, slot_b, qkv)
    qt[...] = flip(qkv[0])
    vt[...] = flip(qkv[2])
    keys = qkv.at[1]
    for i in range(4):
        n = (i + 1) * BLK
        cols = slice(i * BLK, n)
        st = score_block(keys, qt, i)
        top = jnp.max(st, axis=0, keepdims=True)
        p = jnp.exp2(st - top)
        total = jnp.sum(p, axis=0, keepdims=True)
        ot[:, cols] = (dot(vt[:, 0:n], p.astype(BF)) / total).astype(BF)
        lse[:, cols] = jnp.broadcast_to(top + jnp.log2(total), (8, BLK))


def backward_block(i, p, keys_t, values, q, g, gt, delta, dqt, dk, dv):
    n = (i + 1) * BLK
    cols = slice(i * BLK, n)
    dp = dot(values[0:n], gt[:, cols])
    ds = (p * (dp - delta)).astype(BF)
    dqt[:, cols] = (dot(keys_t[:, 0:n], ds) * SCALE).astype(BF)
    add_k = dot(ds, q[cols])
    add_v = dot(p.astype(BF), g[cols])
    if i > 0:
        dk[0 : n - BLK] += add_k[: n - BLK]
        dv[0 : n - BLK] += add_v[: n - BLK]
    dk[n - BLK : n] = add_k[n - BLK :]
    dv[n - BLK : n] = add_v[n - BLK :]


def hand_out(info, outs, dq, dk, dv):
    z = info[0]
    for k in range(4):
        rows = rows_of(z ^ k, BLK)
        outs[k][0] = dq[rows]
        outs[k][1] = (dk[rows] * SCALE).astype(BF)
        outs[k][2] = dv[rows].astype(BF)


def second_kernel(info, *refs):
    slot_a, slot_b, ot1 = refs[0:4], refs[4:8], refs[8]
    outs, g1t = refs[9:13], refs[13]
    qkvg, qt, kt, vt, gt, dq, dk, dv = refs[14:]
    assemble(info, slot_a, slot_b, qkvg)
    q = qkvg[0].astype(F32) + ot1[...].astype(F32).T
    qkvg[0] = q.astype(BF)
    qt[...] = q.T.astype(BF)
    kt[...] = flip(qkvg[1])
    vt[...] = flip(qkvg[2])
    gt[...] = flip(qkvg[3])
    keys, values = qkvg.at[1], qkvg.at[2]
    for i in range(4):
        n = (i + 1) * BLK
        cols = slice(i * BLK, n)
        st = score_block(keys, qt, i)
        top = jnp.max(st, axis=0, keepdims=True)
        p = jnp.exp2(st - top)
        p = p * (1.0 / jnp.sum(p, axis=0, keepdims=True))
        o = dot(vt[:, 0:n], p.astype(BF)).astype(BF)
        delta = jnp.sum(gt[:, cols].astype(F32) * o.astype(F32), axis=0, keepdims=True)
        backward_block(i, p, kt, values, qkvg.at[0], qkvg.at[3], gt, delta, g1t, dk, dv)
    dq[...] = flip(g1t[...])
    hand_out(info, outs, dq, dk, dv)


def first_backward_kernel(info, *refs):
    qkv, ot, lse, gt = refs[0:4]
    outs = refs[4:8]
    g, qt, kt, dqt, dq, dk, dv = refs[8:]
    qt[...] = flip(qkv[0])
    kt[...] = flip(qkv[1])
    g[...] = flip(gt[...])
    keys, values = qkv.at[1], qkv.at[2]
    for i in range(4):
        cols = slice(i * BLK, (i + 1) * BLK)
        st = score_block(keys, qt, i)
        p = jnp.exp2(st - lse[0:1, cols])
        delta = jnp.sum(gt[:, cols].astype(F32) * ot[:, cols].astype(F32), axis=0, keepdims=True)
        backward_block(i, p, kt, values, qkv.at[0], g, gt, delta, dqt, dk, dv)
    dq[...] = flip(dqt[...])
    hand_out(info, outs, dq, dk, dv)


def place_heads(info, slot_a, slot_b, dst):
    z = info[0]
    for k in range(4):
        dst[:, :, head_cols(first_head(z ^ k))] = slot_a[k][...]

        @pl.when(is_edge(z ^ k))
        def _(k=k):
            dst[:, :, head_cols(second_head(z ^ k))] = slot_b[k][...]


def join_second_kernel(info, *refs):
    slot_a, slot_b = refs[0:4], refs[4:8]
    keep, away = refs[8:10]
    (full,) = refs[10:]
    h = info[1]
    place_heads(info, slot_a, slot_b, full)
    keep[...] = full[:, rows_of(h, 128), :]
    away[...] = full[:, rows_of(1 - h, 128), :]


def finish_kernel(info, *refs):
    slot_a, slot_b, keep, came = refs[0:4], refs[4:8], refs[8], refs[9]
    out = refs[10]
    h, s = info[1], info[2]

    @pl.when(s == 0)
    def _():
        place_heads(info, slot_a, slot_b, out)

    @pl.when(s == 1)
    def _():
        row = lax.broadcasted_iota(jnp.int32, (256, 128), 0)
        col = lax.broadcasted_iota(jnp.int32, (256, 128), 1)
        put_own = jnp.where(row == 2 * col + h, 1.0, 0.0).astype(BF)
        put_came = jnp.where(row == 2 * col + 1 - h, 1.0, 0.0).astype(BF)
        for j in range(3):
            out[j] = (dot(put_own, keep[j]) + dot(put_came, came[j])).astype(BF)


def build(n_dp, n_tensor):
    def index(s, d, t):
        return (s * n_dp + d) * n_tensor + t

    def everywhere(rule):
        pairs = []
        for d in range(n_dp):
            for t in range(n_tensor):
                pairs += rule(d, t)
        return pairs

    def send(value, pairs):
        return lax.ppermute(value, AXES, pairs)

    def inward(src, slot, k):
        return everywhere(
            lambda d, t: [(index(src, d, t), index(slot, d ^ k, t))]
            if slot == 0 or (d ^ k) % 4 in (0, 3)
            else []
        )

    def outward(dst, slot, k):
        return [(b, a) for a, b in inward(dst, slot, k)]

    def cross():
        return everywhere(lambda d, t: [(index(1, d, t), index(1, d, t ^ 1))])

    def body(projections, out_grad):
        s = lax.axis_index("section")
        z = lax.axis_index("dp") % 4
        h = lax.axis_index("tensor") % 2
        info = jnp.stack([z, h, s]).astype(jnp.int32)
        local = projections[0]
        rows, cols = local.shape[1:]
        chunk3 = ((3, BLK, HD), BF)
        chunk4 = ((4, BLK, HD), BF)
        half4 = ((4, rows // 2, cols), BF)
        half3 = ((3, rows // 2, cols), BF)
        vm = pltpu.VMEM
        tall, wide = vm((LEN, HD), BF), vm((HD, LEN), BF)
        acc = vm((LEN, HD), F32)

        picked = call(pick_kernel, [chunk3] * 8 + [half4] * 2, [info, local, out_grad])
        own, away = picked[8], picked[9]
        came = send(away, cross())
        first_a = {k: send(picked[k], inward(0, 0, k)) for k in (3, 2, 1)}
        first_b = {k: send(picked[4 + k], inward(0, 1, k)) for k in (3, 2, 1, 0)}
        first_a[0] = picked[0]

        picked2 = call(pick_second_kernel, [chunk4] * 8, [info, own, came])
        second_a = {k: send(picked2[k], inward(1, 0, k)) for k in (3, 2, 1, 0)}
        second_b = {k: send(picked2[4 + k], inward(1, 1, k)) for k in (3, 2, 1)}
        second_b[0] = picked2[4]

        def four(x):
            return [x[k] for k in range(4)]

        qkv, ot, lse = call(
            forward_kernel,
            [((3, LEN, HD), BF), ((HD, LEN), BF), ((8, LEN), F32)],
            [info] + four(first_a) + four(first_b),
            [wide, wide],
        )
        got = call(
            second_kernel,
            [chunk3] * 4 + [((HD, LEN), BF)],
            [info] + four(second_a) + four(second_b) + [ot],
            [vm((4, LEN, HD), BF)] + [wide] * 4 + [tall, acc, acc],
        )
        g1t = got[4]
        back_a = {k: send(got[k], outward(1, 0, k)) for k in (3, 2, 1, 0)}
        back_b = {k: send(got[k], outward(1, 1, k)) for k in (3, 2, 1)}
        back_b[0] = got[0]
        first = call(
            first_backward_kernel,
            [chunk3] * 4,
            [info, qkv, ot, lse, g1t],
            [tall, wide, wide, wide, tall, acc, acc],
        )
        keep, give = call(
            join_second_kernel,
            [half3] * 2,
            [info] + four(back_a) + four(back_b),
            [vm((3, rows, cols), BF)],
        )
        returned = send(give, cross())
        home_a = {k: send(first[k], outward(0, 0, k)) for k in (3, 2, 1)}
        home_b = {k: send(first[k], outward(0, 1, k)) for k in (3, 2, 1, 0)}
        home_a[0] = first[0]
        (out,) = call(
            finish_kernel,
            [((3, rows, cols), BF)],
            [info] + four(home_a) + four(home_b) + [keep, returned],
        )
        return out[None]

    return body


def solution(mesh):
    body = build(mesh.shape["dp"], mesh.shape["tensor"])
    in_specs = (P("section", None, "dp", "tensor"), P("dp", "tensor"))
    out_specs = P("section", None, "dp", "tensor")
    return jax.shard_map(body, mesh=mesh, in_specs=in_specs, out_specs=out_specs, check_vma=False)
```

```python
import math

import jax
import jax.numpy as jnp
from jax import lax
from jax.experimental import pallas as pl
from jax.experimental.pallas import tpu as pltpu
from jax.sharding import PartitionSpec as P

HD = 128
BLK = 256
LEN = 1024
SCALE = 1.0 / math.sqrt(HD)
SCALE2 = SCALE * math.log2(math.e)
AXES = ("section", "dp", "tensor")
BF = jnp.bfloat16
F32 = jnp.float32
VM = pl.BlockSpec(memory_space=pltpu.VMEM)
SM = pl.BlockSpec(memory_space=pltpu.SMEM)


def first_head(z):
    return jnp.where(z > 0, z + 1, 0)


def second_head(z):
    return jnp.where(z == 3, 5, 1)


def is_edge(z):
    return (z == 0) | (z == 3)


def head_cols(head):
    return pl.ds(pl.multiple_of(head * HD, HD), HD)


def rows_of(index, size):
    return pl.ds(pl.multiple_of(index * size, size), size)


def dot(a, b):
    return jnp.dot(a, b, preferred_element_type=F32)


def flip(x):
    return x.astype(F32).T.astype(BF)


def call(kernel, outs, args, scratch=(), flops=0, spec=VM, limit=48):
    return pl.pallas_call(
        kernel,
        out_shape=[jax.ShapeDtypeStruct(s, d) for s, d in outs],
        in_specs=[SM] + [spec] * (len(args) - 1),
        out_specs=[VM] * len(outs),
        scratch_shapes=list(scratch),
        compiler_params=pltpu.CompilerParams(vmem_limit_bytes=limit * 1024 * 1024),
        cost_estimate=pl.CostEstimate(flops=flops, bytes_accessed=4000000, transcendentals=0),
    )(*args)


def selection(rows, cols, odd, spread):
    row = lax.broadcasted_iota(jnp.int32, (rows, cols), 0)
    col = lax.broadcasted_iota(jnp.int32, (rows, cols), 1)
    near, far = (col, row) if spread else (row, col)
    wanted = jnp.where(near < HD, 2 * near + odd, 2 * (near - HD) + 1 - odd)
    return jnp.where(far == wanted, 1.0, 0.0).astype(BF)


def pick_kernel(info, local_hbm, grad_hbm, *refs):
    outs, (local, sems) = refs[:-2], refs[-2:]
    z, s = info[0], info[2]
    copies = [pltpu.make_async_copy(local_hbm.at[j], local.at[j], sems.at[j]) for j in range(3)]
    copies += [pltpu.make_async_copy(grad_hbm, local.at[3], sems.at[3])]
    for copy in copies:
        copy.start()
    for copy in copies:
        copy.wait()

    def fill(out, head, parts):
        for j in range(parts):
            out[j * BLK : (j + 1) * BLK] = local[j, :, head_cols(head)]

    for k in (0, 1):
        heads = first_head(z ^ k), second_head(z ^ k)
        fill(outs[k], jnp.where(s == 0, heads[0], heads[1]), 4)
        fill(outs[2 + k], jnp.where(s == 0, heads[1], heads[0]), 4)

    @pl.when(s == 0)
    def _():
        for k in (2, 3):
            fill(outs[2 + k], first_head(z ^ k), 3)
            fill(outs[4 + k], second_head(z ^ k), 3)

    @pl.when(s == 1)
    def _():
        for k in (2, 3):
            fill(outs[6 + k], first_head(z ^ k), 4)
            fill(outs[8 + k], second_head(z ^ k), 4)


def part_kernel(info, c3, c2, d3, d2, cross1, same1, cross0, same0, own, away, near0, near1):
    z, h, s = info[0], info[1], info[2]
    take = selection(256, 256, h, False)

    def split(chunks):
        for k in range(4):
            rows = rows_of(z ^ k, HD)
            for j in range(4):
                both = dot(take, chunks[k][j * BLK : (j + 1) * BLK]).astype(BF)
                own[j, rows, :] = both[:HD]
                away[j, rows, :] = both[HD:]

    @pl.when(s == 0)
    def _():
        split((cross0, cross1, c2, c3))
        near0[...] = same0[0 : 3 * BLK]
        near1[...] = same1[0 : 3 * BLK]

    @pl.when(s == 1)
    def _():
        split((same0, same1, d2, d3))
        near0[...] = cross0[0 : 3 * BLK]
        near1[...] = cross1[0 : 3 * BLK]


def score_block(keys, qt, i):
    n = (i + 1) * BLK
    st = dot(keys[0:n], qt[:, i * BLK : n]) * SCALE2
    key = lax.broadcasted_iota(jnp.int32, (BLK, BLK), 0)
    qry = lax.broadcasted_iota(jnp.int32, (BLK, BLK), 1)
    tail = jnp.where(key <= qry, st[n - BLK :], -jnp.inf)
    return tail if i == 0 else jnp.concatenate([st[: n - BLK], tail], axis=0)


def backward_block(i, p, keys_t, values, q, g, gt, delta, dqt, dk, dv):
    n = (i + 1) * BLK
    cols = slice(i * BLK, n)
    dp = dot(values[0:n], gt[:, cols])
    ds = (p * (dp - delta)).astype(BF)
    dqt[:, cols] = (dot(keys_t[:, 0:n], ds) * SCALE).astype(BF)
    add_k = dot(ds, q[cols])
    add_v = dot(p.astype(BF), g[cols])
    if i > 0:
        dk[0 : n - BLK] += add_k[: n - BLK]
        dv[0 : n - BLK] += add_v[: n - BLK]
    dk[n - BLK : n] = add_k[n - BLK :]
    dv[n - BLK : n] = add_v[n - BLK :]


def hand_out(info, outs, dq, dk, dv):
    z = info[0]
    for k in range(4):
        rows = rows_of(z ^ k, BLK)
        outs[k][0] = dq[rows]
        outs[k][1] = (dk[rows] * SCALE).astype(BF)
        outs[k][2] = dv[rows].astype(BF)


def forward_kernel(info, a3, a2, b3, b2, near0, near1, qkv, ot, lse, qt, vt):
    z, s = info[0], info[2]

    def join(chunks):
        for k in range(4):
            for j in range(3):
                qkv[j, rows_of(z ^ k, BLK), :] = chunks[k][j * BLK : (j + 1) * BLK]

    @pl.when(s == 0)
    def _():
        join((near0, near1, a2, a3))

    @pl.when(s == 1)
    def _():
        join((near0, near1, b2, b3))

    qt[...] = flip(qkv[0])
    vt[...] = flip(qkv[2])
    keys = qkv.at[1]
    for i in range(4):
        n = (i + 1) * BLK
        cols = slice(i * BLK, n)
        st = score_block(keys, qt, i)
        top = jnp.max(st, axis=0, keepdims=True)
        p = jnp.exp2(st - top)
        total = jnp.sum(p, axis=0, keepdims=True)
        ot[:, cols] = (dot(vt[:, 0:n], p.astype(BF)) / total).astype(BF)
        lse[:, cols] = jnp.broadcast_to(top + jnp.log2(total), (8, BLK))


def second_kernel(info, own, came, ot1, keep, give, g1t, qkvg, qt, kt, vt, gt, dq, dk, dv):
    h = info[1]

    def block(b, part):
        return pl.ds(pl.multiple_of(b * BLK + part * HD, HD), HD)

    for j in range(4):
        for b in range(4):
            qkvg[j, block(b, h), :] = own[j, b * HD : (b + 1) * HD]
            qkvg[j, block(b, 1 - h), :] = came[j, b * HD : (b + 1) * HD]
    q = qkvg[0].astype(F32) + ot1[...].astype(F32).T
    qkvg[0] = q.astype(BF)
    qt[...] = q.T.astype(BF)
    kt[...] = flip(qkvg[1])
    vt[...] = flip(qkvg[2])
    gt[...] = flip(qkvg[3])
    keys, values = qkvg.at[1], qkvg.at[2]
    for i in range(4):
        n = (i + 1) * BLK
        cols = slice(i * BLK, n)
        st = score_block(keys, qt, i)
        top = jnp.max(st, axis=0, keepdims=True)
        p = jnp.exp2(st - top)
        p = p * (1.0 / jnp.sum(p, axis=0, keepdims=True))
        o = dot(vt[:, 0:n], p.astype(BF)).astype(BF)
        delta = jnp.sum(gt[:, cols].astype(F32) * o.astype(F32), axis=0, keepdims=True)
        backward_block(i, p, kt, values, qkvg.at[0], qkvg.at[3], gt, delta, g1t, dk, dv)
    dq[...] = flip(g1t[...])
    for b in range(4):
        rows = slice(b * HD, (b + 1) * HD)
        for out, part in ((keep, h), (give, 1 - h)):
            out[0, rows] = dq[block(b, part)]
            out[1, rows] = (dk[block(b, part)] * SCALE).astype(BF)
            out[2, rows] = dv[block(b, part)].astype(BF)


def first_backward_kernel(info, qkv, ot, lse, gt, *refs):
    outs = refs[0:4]
    g, qt, kt, dqt, dq, dk, dv = refs[4:]
    z = info[0]
    qt[...] = flip(qkv[0])
    kt[...] = flip(qkv[1])
    g[...] = flip(gt[...])
    keys, values = qkv.at[1], qkv.at[2]
    for i in range(4):
        cols = slice(i * BLK, (i + 1) * BLK)
        st = score_block(keys, qt, i)
        p = jnp.exp2(st - lse[0:1, cols])
        delta = jnp.sum(gt[:, cols].astype(F32) * ot[:, cols].astype(F32), axis=0, keepdims=True)
        backward_block(i, p, kt, values, qkv.at[0], g, gt, delta, dqt, dk, dv)
    dq[...] = flip(dqt[...])
    for k in range(4):
        rows = rows_of(z ^ k, BLK)
        outs[k][0] = dq[rows]
        outs[k][1] = (dk[rows] * SCALE).astype(BF)
        outs[k][2] = dv[rows].astype(BF)


def weave_kernel(info, keep, came, d0, d1, same0, same1, cross0, cross1, out2, out3):
    z, h, s = info[0], info[1], info[2]
    put = selection(256, 256, h, True)

    def weave(out, k):
        rows = rows_of(z ^ k, HD)
        for j in range(3):
            both = jnp.concatenate([keep[j, rows, :], came[j, rows, :]], axis=0)
            out[j] = dot(put, both).astype(BF)

    @pl.when(s == 0)
    def _():
        same0[...] = d0[...]
        same1[...] = d1[...]
        weave(cross0, 0)
        weave(cross1, 1)

    @pl.when(s == 1)
    def _():
        cross0[...] = d0[...]
        cross1[...] = d1[...]
        weave(same0, 0)
        weave(same1, 1)

    weave(out2, 2)
    weave(out3, 3)


def finish_kernel(info, a3, a2, b3, b2, c3, c2, d3, d2, *refs):
    cross1, same1, cross0, same0, out = refs
    z, s = info[0], info[2]

    def place(slot_a, slot_b):
        for k in range(4):
            out[:, :, head_cols(first_head(z ^ k))] = slot_a[k][...]

            @pl.when(is_edge(z ^ k))
            def _(k=k):
                out[:, :, head_cols(second_head(z ^ k))] = slot_b[k][...]

    @pl.when(s == 0)
    def _():
        place((same0, same1, a2, a3), (cross0, cross1, b2, b3))

    @pl.when(s == 1)
    def _():
        place((cross0, cross1, c2, c3), (same0, same1, d2, d3))


def build(n_dp, n_tensor):
    def index(s, d, t):
        return (s * n_dp + d) * n_tensor + t

    def everywhere(rule):
        pairs = []
        for d in range(n_dp):
            for t in range(n_tensor):
                pairs += rule(d, t)
        return pairs

    def send(value, pairs):
        return lax.ppermute(value, AXES, pairs)

    def inward(src, slot, k):
        return everywhere(
            lambda d, t: [(index(src, d, t), index(slot, d ^ k, t))]
            if slot == 0 or (d ^ k) % 4 in (0, 3)
            else []
        )

    def outward(dst, slot, k):
        return [(b, a) for a, b in inward(dst, slot, k)]

    def cross():
        return everywhere(
            lambda d, t: [
                (index(c, d, t), index(c, d, t ^ 1)) for c in range(2) if c == 0 or d % 4 in (0, 3)
            ]
        )

    def body(projections, out_grad):
        s = lax.axis_index("section")
        z = lax.axis_index("dp") % 4
        h = lax.axis_index("tensor") % 2
        info = jnp.stack([z, h, s]).astype(jnp.int32)
        local = projections[0]
        rows, cols = local.shape[1:]
        small, large = ((3 * BLK, HD), BF), ((4 * BLK, HD), BF)
        chunk = ((3, BLK, HD), BF)
        vm = pltpu.VMEM
        tall, wide = vm((LEN, HD), BF), vm((HD, LEN), BF)
        acc = vm((LEN, HD), F32)

        same0, same1, cross0, cross1, a2, a3, b2, b3, c2, c3, d2, d3 = call(
            pick_kernel,
            [large] * 4 + [small] * 4 + [large] * 4,
            [info, local, out_grad],
            [vm((4, rows, cols), BF), pltpu.SemaphoreType.DMA((4,))],
            spec=pl.BlockSpec(memory_space=pl.ANY),
            limit=51,
        )
        c3 = send(c3, inward(1, 0, 3))
        c2 = send(c2, inward(1, 0, 2))
        d3 = send(d3, inward(1, 1, 3))
        d2 = send(d2, inward(1, 1, 2))
        same1 = send(same1, inward(0, 0, 1) + inward(1, 1, 1))
        cross1 = send(cross1, inward(0, 1, 1) + inward(1, 0, 1))
        cross0 = send(cross0, inward(0, 1, 0) + inward(1, 0, 0))
        own, away, near0, near1 = call(
            part_kernel,
            [((4, 4 * HD, HD), BF)] * 2 + [small] * 2,
            [info, c3, c2, d3, d2, cross1, same1, cross0, same0],
        )
        came = send(away, cross())
        a3 = send(a3, inward(0, 0, 3))
        a2 = send(a2, inward(0, 0, 2))
        b3 = send(b3, inward(0, 1, 3))
        b2 = send(b2, inward(0, 1, 2))
        qkv, ot, lse = call(
            forward_kernel,
            [((3, LEN, HD), BF), ((HD, LEN), BF), ((8, LEN), F32)],
            [info, a3, a2, b3, b2, near0, near1],
            [wide, wide],
        )
        keep, give, g1t = call(
            second_kernel,
            [((3, 4 * HD, HD), BF)] * 2 + [((HD, LEN), BF)],
            [info, own, came, ot],
            [vm((4, LEN, HD), BF)] + [wide] * 4 + [tall, acc, acc],
        )
        came = send(give, cross())
        d0, d1, d2, d3 = call(
            first_backward_kernel,
            [chunk] * 4,
            [info, qkv, ot, lse, g1t],
            [tall, wide, wide, wide, tall, acc, acc],
        )
        a3 = send(d3, outward(0, 0, 3))
        a2 = send(d2, outward(0, 0, 2))
        b3 = send(d3, outward(0, 1, 3))
        b2 = send(d2, outward(0, 1, 2))
        same0, same1, cross0, cross1, c2, c3 = call(
            weave_kernel, [chunk] * 6, [info, keep, came, d0, d1]
        )
        d3 = send(c3, outward(1, 1, 3))
        d2 = send(c2, outward(1, 1, 2))
        c3 = send(c3, outward(1, 0, 3))
        c2 = send(c2, outward(1, 0, 2))
        same1 = send(same1, outward(0, 0, 1) + outward(1, 1, 1))
        cross1 = send(cross1, outward(0, 1, 1) + outward(1, 0, 1))
        cross0 = send(cross0, outward(0, 1, 0) + outward(1, 0, 0))
        (out,) = call(
            finish_kernel,
            [((3, rows, cols), BF)],
            [info, a3, a2, b3, b2, c3, c2, d3, d2, cross1, same1, cross0, same0],
        )
        return out[None]

    return body


def solution(mesh):
    body = build(mesh.shape["dp"], mesh.shape["tensor"])
    in_specs = (P("section", None, "dp", "tensor"), P("dp", "tensor"))
    out_specs = P("section", None, "dp", "tensor")
    return jax.shard_map(body, mesh=mesh, in_specs=in_specs, out_specs=out_specs, check_vma=False)
```

```python
import math

import jax
import jax.numpy as jnp
from jax import lax
from jax.experimental import pallas as pl
from jax.experimental.pallas import tpu as pltpu
from jax.sharding import PartitionSpec as P

HD = 128
BLK = 256
LEN = 1024
SCALE = 1.0 / math.sqrt(HD)
SCALE2 = SCALE * math.log2(math.e)
AXES = ("section", "dp", "tensor")
BF = jnp.bfloat16
F32 = jnp.float32
VM = pl.BlockSpec(memory_space=pltpu.VMEM)
SM = pl.BlockSpec(memory_space=pltpu.SMEM)
ANY = pl.BlockSpec(memory_space=pl.ANY)


def first_head(z):
    return 2 * z - jnp.where(z > 0, 1, 0)


def second_head(z):
    return jnp.where(z == 2, 4, 2)


def is_inner(z):
    return (z == 1) | (z == 2)


def head_cols(head):
    return pl.ds(pl.multiple_of(head * HD, HD), HD)


def rows_of(index, size):
    return pl.ds(pl.multiple_of(index * size, size), size)


def dot(a, b):
    return jnp.dot(a, b, preferred_element_type=F32)


def flip(x):
    return x.astype(F32).T.astype(BF)


def call(kernel, outs, args, scratch=(), flops=0, spec=VM, limit=48, after=()):
    first = len(args)

    def body(*refs):
        kernel(*refs[:first], *refs[first + len(after) :])

    return pl.pallas_call(
        body,
        out_shape=[jax.ShapeDtypeStruct(s, d) for s, d in outs],
        in_specs=[SM] + [spec] * (first - 1) + [ANY] * len(after),
        out_specs=[VM] * len(outs),
        scratch_shapes=list(scratch),
        compiler_params=pltpu.CompilerParams(vmem_limit_bytes=int(limit * 1024 * 1024)),
        cost_estimate=pl.CostEstimate(flops=flops, bytes_accessed=4000000, transcendentals=0),
    )(*args, *after)


CHUNK = 3 * BLK + HD


def selection(rows, cols, odd):
    row = lax.broadcasted_iota(jnp.int32, (rows, cols), 0)
    col = lax.broadcasted_iota(jnp.int32, (rows, cols), 1)
    return jnp.where(col == 2 * row + odd, 1.0, 0.0).astype(BF)


def fetch(local_hbm, grad_hbm, local, sems):
    copies = [pltpu.make_async_copy(local_hbm.at[j], local.at[j], sems.at[j]) for j in range(3)]
    copies += [pltpu.make_async_copy(grad_hbm, local.at[3], sems.at[3])]
    for copy in copies:
        copy.start()
    for copy in copies:
        copy.wait()


def fill_first(out, start, local, grad, head):
    cols = head_cols(head)
    for j in range(3):
        out[start + j * BLK : start + (j + 1) * BLK] = local[j, :, cols]
    out[start + 3 * BLK : start + CHUNK] = grad[:, cols]


def pick_far_kernel(info, local_hbm, grad_hbm, away, a3, a2, b3, b2, local, sems, grad):
    z, h, s = info[0], info[1], info[2]
    fetch(local_hbm, grad_hbm, local, sems)

    @pl.when(s == 0)
    def _():
        grad[...] = dot(selection(128, 256, h), local[3]).astype(BF)
        fill_first(a3, 0, local, grad, first_head(z ^ 3))
        fill_first(a2, 0, local, grad, first_head(z ^ 2))
        fill_first(b3, 0, local, grad, second_head(z ^ 3))
        fill_first(b2, 0, local, grad, second_head(z ^ 2))

    @pl.when(s == 1)
    def _():
        for j in range(4):
            away[j] = dot(selection(128, 256, 1 - h), local[j]).astype(BF)


def pick_near_kernel(info, local_hbm, grad_hbm, stash, local, sems, grad):
    z, h, s = info[0], info[1], info[2]
    fetch(local_hbm, grad_hbm, local, sems)

    @pl.when(s == 0)
    def _():
        grad[...] = dot(selection(128, 256, h), local[3]).astype(BF)
        for k in range(2):
            fill_first(stash, k * CHUNK, local, grad, second_head(z ^ k))
            fill_first(stash, (2 + k) * CHUNK, local, grad, first_head(z ^ k))

    @pl.when(s == 1)
    def _():
        for j in range(3):
            own = dot(selection(128, 256, h), local[j]).astype(BF)
            for head in range(6):
                start = (head * 3 + j) * HD
                stash[start : start + HD] = own[:, head * HD : (head + 1) * HD]


def pick_second_kernel(info, stash, came, *outs):
    z, h, s = info[0], info[1], info[2]

    def fill(out, head):
        cols = head_cols(head)
        for j in range(3):
            mine = pl.ds(pl.multiple_of(j * BLK + h * HD, HD), HD)
            theirs = pl.ds(pl.multiple_of(j * BLK + (1 - h) * HD, HD), HD)
            out[mine, :] = stash[rows_of(head * 3 + j, HD), :]
            out[theirs, :] = came[j, :, cols]
        out[3 * BLK :] = came[3, :, cols]

    @pl.when(s == 0)
    def _():
        for k in range(4):
            outs[k][...] = stash[k * CHUNK : (k + 1) * CHUNK]

    @pl.when(s == 1)
    def _():
        for k in range(2):
            fill(outs[k], first_head(z ^ k))
            fill(outs[2 + k], second_head(z ^ k))
            fill(outs[4 + k], first_head(z ^ (2 + k)))
            fill(outs[6 + k], second_head(z ^ (2 + k)))


def score_block(keys, qt, i):
    n = (i + 1) * BLK
    st = dot(keys[0:n], qt[:, i * BLK : n]) * SCALE2
    key = lax.broadcasted_iota(jnp.int32, (BLK, BLK), 0)
    qry = lax.broadcasted_iota(jnp.int32, (BLK, BLK), 1)
    tail = jnp.where(key <= qry, st[n - BLK :], -jnp.inf)
    return tail if i == 0 else jnp.concatenate([st[: n - BLK], tail], axis=0)


def backward_block(i, p, keys_t, values, q, g, gt, delta, dqt, dk, dv):
    n = (i + 1) * BLK
    cols = slice(i * BLK, n)
    dp = dot(values[0:n], gt[:, cols])
    ds = (p * (dp - delta)).astype(BF)
    dqt[:, cols] = (dot(keys_t[:, 0:n], ds) * SCALE).astype(BF)
    add_k = dot(ds, q[cols])
    add_v = dot(p.astype(BF), g[cols])
    if i > 0:
        dk[0 : n - BLK] += add_k[: n - BLK]
        dv[0 : n - BLK] += add_v[: n - BLK]
    dk[n - BLK : n] = add_k[n - BLK :]
    dv[n - BLK : n] = add_v[n - BLK :]


def hand_out(info, outs, dq, dk, dv):
    z = info[0]
    for k in range(4):
        rows = rows_of(z ^ k, BLK)
        outs[k][0] = dq[rows]
        outs[k][1] = (dk[rows] * SCALE).astype(BF)
        outs[k][2] = dv[rows].astype(BF)


def backward_block(i, p, keys_t, values, q, g, gt, delta, dqt, dk, dv):
    n = (i + 1) * BLK
    cols = slice(i * BLK, n)
    dp = dot(values[0:n], gt[:, cols])
    ds = (p * (dp - delta)).astype(BF)
    dqt[:, cols] = (dot(keys_t[:, 0:n], ds) * SCALE).astype(BF)
    add_k = dot(ds, q[cols])
    add_v = dot(p.astype(BF), g[cols])
    if i > 0:
        dk[0 : n - BLK] += add_k[: n - BLK]
        dv[0 : n - BLK] += add_v[: n - BLK]
    dk[n - BLK : n] = add_k[n - BLK :]
    dv[n - BLK : n] = add_v[n - BLK :]


def main_kernel(info, *refs):
    a3, a2, b3, b2, x3, x0, x1, same1, x2, d3, d2, here = refs[0:12]
    keep, give, out0, out1, to_a3, to_a2, to_b3, to_b2 = refs[12:20]
    qkv, qkvg, ot1, g1, qt, kt, vt, gt, p1, dq, dk, dv = refs[20:]
    z, h, s = info[0], info[1], info[2]

    def join(first, second):
        for k in range(4):
            rows = rows_of(z ^ k, BLK)
            for j in range(3):
                qkv[j, rows, :] = first[k][j * BLK : (j + 1) * BLK]
                qkvg[j, rows, :] = second[k][j * BLK : (j + 1) * BLK]
            for part, chunk in ((h, first[k]), (1 - h, second[k])):
                at = pl.ds(pl.multiple_of((z ^ k) * BLK + part * HD, HD), HD)
                qkvg[3, at, :] = chunk[3 * BLK :]

    @pl.when(s == 0)
    def _():
        join((here, same1, a2, a3), (x0, x1, x2, x3))

    @pl.when(s == 1)
    def _():
        join((x0, x1, b2, b3), (here, same1, d2, d3))

    qt[...] = flip(qkv[0])
    vt[...] = flip(qkv[2])
    keys = qkv.at[1]
    for i in range(4):
        n = (i + 1) * BLK
        cols = slice(i * BLK, n)
        st = score_block(keys, qt, i)
        top = jnp.max(st, axis=0, keepdims=True)
        p = jnp.exp2(st - top)
        p = p * (1.0 / jnp.sum(p, axis=0, keepdims=True))
        p1[0:n, cols] = p
        ot1[:, cols] = dot(vt[:, 0:n], p.astype(BF)).astype(BF)

    q = qkvg[0].astype(F32) + ot1[...].astype(F32).T
    qkvg[0] = q.astype(BF)
    qt[...] = q.T.astype(BF)
    kt[...] = flip(qkvg[1])
    vt[...] = flip(qkvg[2])
    gt[...] = flip(qkvg[3])
    keys, values = qkvg.at[1], qkvg.at[2]
    for i in range(4):
        n = (i + 1) * BLK
        cols = slice(i * BLK, n)
        st = score_block(keys, qt, i)
        top = jnp.max(st, axis=0, keepdims=True)
        p = jnp.exp2(st - top)
        p = p * (1.0 / jnp.sum(p, axis=0, keepdims=True))
        o = dot(vt[:, 0:n], p.astype(BF)).astype(BF)
        delta = jnp.sum(gt[:, cols].astype(F32) * o.astype(F32), axis=0, keepdims=True)
        backward_block(i, p, kt, values, qkvg.at[0], qkvg.at[3], gt, delta, g1, dk, dv)
    dq[...] = flip(g1[...])

    def block(b, part):
        return pl.ds(pl.multiple_of(b * BLK + part * HD, HD), HD)

    for b in range(4):
        rows = slice(b * HD, (b + 1) * HD)
        for out, part in ((keep, h), (give, 1 - h)):
            out[0, rows] = dq[block(b, part)]
            out[1, rows] = (dk[block(b, part)] * SCALE).astype(BF)
            out[2, rows] = dv[block(b, part)].astype(BF)

    kt[...] = flip(qkv[1])
    values = qkv.at[2]
    for i in range(4):
        cols = slice(i * BLK, (i + 1) * BLK)
        p = p1[0 : (i + 1) * BLK, cols]
        delta = jnp.sum(g1[:, cols].astype(F32) * ot1[:, cols].astype(F32), axis=0, keepdims=True)
        backward_block(i, p, kt, values, qkv.at[0], dq, g1, delta, gt, dk, dv)
    dq[...] = flip(gt[...])

    def hand_out(outs):
        for k, out in enumerate(outs):
            rows = rows_of(z ^ k, BLK)
            out[0] = dq[rows]
            out[1] = (dk[rows] * SCALE).astype(BF)
            out[2] = dv[rows].astype(BF)

    @pl.when(s == 0)
    def _():
        hand_out((out0, out1, to_a2, to_a3))

    @pl.when(s == 1)
    def _():
        hand_out((out0, out1, to_b2, to_b3))


def weave_kernel(info, keep, came, d0, d1, x3, x2, c3, c2, x1, same1, x0, here):
    z, h, s = info[0], info[1], info[2]
    row = lax.broadcasted_iota(jnp.int32, (256, 256), 0)
    col = lax.broadcasted_iota(jnp.int32, (256, 256), 1)
    wanted = jnp.where(col < HD, 2 * col + h, 2 * (col - HD) + 1 - h)
    put = jnp.where(row == wanted, 1.0, 0.0).astype(BF)

    def weave(out, k):
        rows = rows_of(z ^ k, HD)
        for j in range(3):
            both = jnp.concatenate([keep[j, rows, :], came[j, rows, :]], axis=0)
            out[j] = dot(put, both).astype(BF)

    @pl.when(s == 0)
    def _():
        here[...] = d0[...]
        same1[...] = d1[...]
        for k, out in enumerate((x0, x1, x2, x3)):
            weave(out, k)

    @pl.when(s == 1)
    def _():
        x0[...] = d0[...]
        x1[...] = d1[...]
        for k, out in enumerate((here, same1, c2, c3)):
            weave(out, k)


def finish_kernel(info, *refs):
    a3, a2, b3, b2, x3, x0, x1, same1, x2, c3, c2, here, out = refs
    z, s = info[0], info[2]

    def place(slot_a, slot_b):
        for k in range(4):
            out[:, :, head_cols(first_head(z ^ k))] = slot_a[k][...]

            @pl.when(is_inner(z ^ k))
            def _(k=k):
                out[:, :, head_cols(second_head(z ^ k))] = slot_b[k][...]

    @pl.when(s == 0)
    def _():
        place((here, same1, a2, a3), (x0, x1, b2, b3))

    @pl.when(s == 1)
    def _():
        place((x0, x1, x2, x3), (here, same1, c2, c3))


def build(n_dp, n_tensor):
    def index(s, d, t):
        return (s * n_dp + d) * n_tensor + t

    def everywhere(rule):
        pairs = []
        for d in range(n_dp):
            for t in range(n_tensor):
                pairs += rule(d, t)
        return pairs

    def send(value, pairs):
        return lax.ppermute(value, AXES, pairs)

    def inward(src, slot, k):
        return everywhere(
            lambda d, t: [(index(src, d, t), index(slot, d ^ k, t))]
            if slot == 0 or (d ^ k) % 4 in (1, 2)
            else []
        )

    def outward(dst, slot, k):
        return [(b, a) for a, b in inward(dst, slot, k)]

    def swap_lines(value, cores):
        return send(
            value,
            everywhere(
                lambda d, t: [
                    (index(c, d, t), index(c, d, t ^ 1))
                    for c in cores
                    if c == 1 and len(cores) == 1 or c == 0 or d % 4 in (1, 2)
                ]
            ),
        )

    def body(projections, out_grad):
        s = lax.axis_index("section")
        z = lax.axis_index("dp") % 4
        h = lax.axis_index("tensor") % 2
        info = jnp.stack([z, h, s]).astype(jnp.int32)
        local = projections[0]
        rows, cols = local.shape[1:]
        half = ((4, rows // 2, cols), BF)
        chunk_in = ((CHUNK, HD), BF)
        chunk = ((3, BLK, HD), BF)
        vm = pltpu.VMEM
        tall, wide = vm((LEN, HD), BF), vm((HD, LEN), BF)
        acc = vm((LEN, HD), F32)

        inputs = [info] + [
            pltpu.with_memory_space_constraint(x, pltpu.HBM) for x in (local, out_grad)
        ]
        hbm = pl.BlockSpec(memory_space=pltpu.HBM)
        staging = [vm((4, rows, cols), BF), pltpu.SemaphoreType.DMA((4,)), vm((HD, cols), BF)]
        away, a3, a2, b3, b2 = call(
            pick_far_kernel, [half] + [chunk_in] * 4, inputs, staging, spec=hbm
        )
        came = swap_lines(away, (1,))
        a3 = send(a3, inward(0, 0, 3))
        a2 = send(a2, inward(0, 0, 2))
        b3 = send(b3, inward(0, 1, 3))
        b2 = send(b2, inward(0, 1, 2))
        (stash,) = call(
            pick_near_kernel, [((4 * CHUNK, HD), BF)], inputs, staging, 0, hbm
        )
        x0, x1, here, same1, x2, x3, d2, d3 = call(
            pick_second_kernel, [chunk_in] * 8, [info, stash, came]
        )
        x3 = send(x3, inward(1, 0, 3))
        x2 = send(x2, inward(1, 0, 2))
        d3 = send(d3, inward(1, 1, 3))
        d2 = send(d2, inward(1, 1, 2))
        x1 = send(x1, inward(0, 1, 1) + inward(1, 0, 1))
        same1 = send(same1, inward(0, 0, 1) + inward(1, 1, 1))
        x0 = send(x0, inward(0, 1, 0) + inward(1, 0, 0))
        keep, give, d0, d1, a3, a2, b3, b2 = call(
            main_kernel,
            [((3, 4 * HD, HD), BF)] * 2 + [chunk] * 6,
            [info, a3, a2, b3, b2, x3, x0, x1, same1, x2, d3, d2, here],
            [vm((3, LEN, HD), BF), vm((4, LEN, HD), BF)]
            + [wide] * 6
            + [vm((LEN, LEN), F32), tall, acc, acc],
        )
        came = swap_lines(give, (0, 1))
        a3 = send(a3, outward(0, 0, 3))
        a2 = send(a2, outward(0, 0, 2))
        b3 = send(b3, outward(0, 1, 3))
        b2 = send(b2, outward(0, 1, 2))
        x3, x2, c3, c2, x1, same1, x0, here = call(
            weave_kernel, [chunk] * 8, [info, keep, came, d0, d1]
        )
        x3 = send(x3, outward(1, 0, 3))
        x2 = send(x2, outward(1, 0, 2))
        c3 = send(c3, outward(1, 1, 3))
        c2 = send(c2, outward(1, 1, 2))
        x1 = send(x1, outward(0, 1, 1) + outward(1, 0, 1))
        same1 = send(same1, outward(0, 0, 1) + outward(1, 1, 1))
        x0 = send(x0, outward(0, 1, 0) + outward(1, 0, 0))
        (out,) = call(
            finish_kernel,
            [((3, rows, cols), BF)],
            [info, a3, a2, b3, b2, x3, x0, x1, same1, x2, c3, c2, here],
        )
        return out[None]

    return body


def solution(mesh):
    body = build(mesh.shape["dp"], mesh.shape["tensor"])
    in_specs = (P("section", None, "dp", "tensor"), P("dp", "tensor"))
    out_specs = P("section", None, "dp", "tensor")
    return jax.shard_map(body, mesh=mesh, in_specs=in_specs, out_specs=out_specs, check_vma=False)
```

```python
import math

import jax
import jax.numpy as jnp
from jax import lax
from jax.experimental import pallas as pl
from jax.experimental.pallas import tpu as pltpu
from jax.sharding import PartitionSpec as P

HD = 128
BLK = 256
LEN = 1024
SCALE = 1.0 / math.sqrt(HD)
SCALE2 = SCALE * math.log2(math.e)
AXES = ("section", "dp", "tensor")
BF = jnp.bfloat16
F32 = jnp.float32
VM = pl.BlockSpec(memory_space=pltpu.VMEM)
SM = pl.BlockSpec(memory_space=pltpu.SMEM)


def first_head(z):
    return 2 * z - jnp.where(z > 0, 1, 0)


def second_head(z):
    return jnp.where(z == 2, 4, 2)


def is_inner(z):
    return (z == 1) | (z == 2)


def head_cols(head):
    return pl.ds(pl.multiple_of(head * HD, HD), HD)


def rows_of(index, size):
    return pl.ds(pl.multiple_of(index * size, size), size)


def dot_nt(a, b):
    return lax.dot_general(a, b, (((1,), (1,)), ((), ())), preferred_element_type=F32)


def dot(a, b):
    return jnp.dot(a, b, preferred_element_type=F32)


def flip(x):
    return x.T


def call(kernel, outs, args, scratch=(), flops=0, spec=VM, out_spec=VM):
    return pl.pallas_call(
        kernel,
        out_shape=[jax.ShapeDtypeStruct(s, d) for s, d in outs],
        in_specs=[SM] + [spec] * (len(args) - 1),
        out_specs=[out_spec] * len(outs),
        scratch_shapes=list(scratch),
        compiler_params=pltpu.CompilerParams(vmem_limit_bytes=48 * 1024 * 1024),
        cost_estimate=pl.CostEstimate(flops=flops, bytes_accessed=4000000, transcendentals=0),
    )(*args)


CHUNK = 3 * BLK + HD


def selection(rows, cols, odd):
    row = lax.broadcasted_iota(jnp.int32, (rows, cols), 0)
    col = lax.broadcasted_iota(jnp.int32, (rows, cols), 1)
    return jnp.where(col == 2 * row + odd, 1.0, 0.0).astype(BF)


def fill_first(out, start, local, grad, head):
    cols = head_cols(head)
    for j in range(3):
        out[start + j * BLK : start + (j + 1) * BLK] = local[j, :, cols]
    out[start + 3 * BLK : start + CHUNK] = grad[:, cols]


def pick_far_kernel(info, local_hbm, grad_hbm, away, a2, a3, a1, near, local, sems, grad):
    z, h, s = info[0], info[1], info[2]
    sources = [grad_hbm] + [local_hbm.at[j] for j in range(3)]
    copies = [
        pltpu.make_async_copy(source, local.at[i], sems.at[i]) for i, source in enumerate(sources)
    ]
    for copy in copies:
        copy.start()

    @pl.when(s == 0)
    def _():
        copies[0].wait()
        grad[...] = dot(selection(128, 256, h), local[0]).astype(BF)
        for copy in copies[1:]:
            copy.wait()
        rows = local.at[1:4]
        fill_first(a3, 0, rows, grad, first_head(z ^ 3))
        fill_first(a2, 0, rows, grad, first_head(z ^ 2))
        fill_first(a1, 0, rows, grad, first_head(z ^ 1))
        for k in range(4):
            fill_first(near, k * CHUNK, rows, grad, second_head(z ^ k))
        fill_first(near, 4 * CHUNK, rows, grad, first_head(z))

    @pl.when(s == 1)
    def _():
        take = selection(128, 256, 1 - h)
        for i, copy in enumerate(copies):
            copy.wait()
            away[(i - 1) % 4] = dot(take, local[i]).astype(BF)


def pick_own_kernel(info, local_hbm, stash, local, sems):
    h, s = info[1], info[2]

    @pl.when(s == 1)
    def _():
        copies = [
            pltpu.make_async_copy(local_hbm.at[j], local.at[j], sems.at[j]) for j in range(3)
        ]
        for copy in copies:
            copy.start()
        for j, copy in enumerate(copies):
            copy.wait()
            own = dot(selection(128, 256, h), local[j]).astype(BF)
            for head in range(6):
                start = (head * 3 + j) * HD
                stash[start : start + HD] = own[:, head * HD : (head + 1) * HD]


def pick_second_kernel(info, near, stash, came, *outs):
    z, h, s = info[0], info[1], info[2]

    def fill(out, head):
        cols = head_cols(head)
        for j in range(3):
            mine = pl.ds(pl.multiple_of(j * BLK + h * HD, HD), HD)
            theirs = pl.ds(pl.multiple_of(j * BLK + (1 - h) * HD, HD), HD)
            out[mine, :] = stash[rows_of(head * 3 + j, HD), :]
            out[theirs, :] = came[j, :, cols]
        out[3 * BLK :] = came[3, :, cols]

    @pl.when(s == 0)
    def _():
        for k in range(5):
            outs[k][...] = near[k * CHUNK : (k + 1) * CHUNK]

    @pl.when(s == 1)
    def _():
        for k in range(4):
            fill(outs[k], first_head(z ^ k))
            fill(outs[4 + k], second_head(z ^ k))


def score_block(keys, q, i):
    n = (i + 1) * BLK
    st = dot_nt(keys[0:n], q[i * BLK : n]) * SCALE2
    key = lax.broadcasted_iota(jnp.int32, (BLK, BLK), 0)
    qry = lax.broadcasted_iota(jnp.int32, (BLK, BLK), 1)
    tail = jnp.where(key <= qry, st[n - BLK :], -jnp.inf)
    return tail if i == 0 else jnp.concatenate([st[: n - BLK], tail], axis=0)


def backward_block(i, p, dp, delta, keys_t, q, g, dqt, dk, dv):
    n = (i + 1) * BLK
    cols = slice(i * BLK, n)
    ds = (p * (dp - delta)).astype(BF)
    dqt[:, cols] = (dot(keys_t[:, 0:n], ds) * SCALE).astype(BF)
    add_k = dot(ds, q[cols])
    add_v = dot(p.astype(BF), g[cols])
    if i > 0:
        dk[0 : n - BLK] += add_k[: n - BLK]
        dv[0 : n - BLK] += add_v[: n - BLK]
    dk[n - BLK : n] = add_k[n - BLK :]
    dv[n - BLK : n] = add_v[n - BLK :]


def hand_out(info, outs, dq, dk, dv):
    z = info[0]
    for k in range(4):
        rows = rows_of(z ^ k, BLK)
        outs[k][0] = dq[rows]
        outs[k][1] = (dk[rows] * SCALE).astype(BF)
        outs[k][2] = dv[rows].astype(BF)


def backward_block(i, p, dp, delta, keys_t, q, g, dqt, dk, dv):
    n = (i + 1) * BLK
    cols = slice(i * BLK, n)
    ds = (p * (dp - delta)).astype(BF)
    dqt[:, cols] = (dot(keys_t[:, 0:n], ds) * SCALE).astype(BF)
    add_k = dot(ds, q[cols])
    add_v = dot(p.astype(BF), g[cols])
    if i > 0:
        dk[0 : n - BLK] += add_k[: n - BLK]
        dv[0 : n - BLK] += add_v[: n - BLK]
    dk[n - BLK : n] = add_k[n - BLK :]
    dv[n - BLK : n] = add_v[n - BLK :]


def main_kernel(info, *refs):
    a2, a3, a1, x3, x0, x1, d1, x2, d2, d3, here = refs[0:11]
    keep, give, out0, out1, out2, out3 = refs[11:17]
    first, second, ot1, g1, kt1, vt1, kt2, dqt1, p1, dq1, dq2, dk1, dv1, dk2, dv2 = refs[17:]
    z, h, s = info[0], info[1], info[2]

    def join(from_first, from_second):
        for k in range(4):
            rows = rows_of(z ^ k, BLK)
            for j in range(3):
                first[j, rows, :] = from_first[k][j * BLK : (j + 1) * BLK]
                second[j, rows, :] = from_second[k][j * BLK : (j + 1) * BLK]
            for part, chunk in ((h, from_first[k]), (1 - h, from_second[k])):
                at = pl.ds(pl.multiple_of((z ^ k) * BLK + part * HD, HD), HD)
                second[3, at, :] = chunk[3 * BLK :]

    @pl.when(s == 0)
    def _():
        join((here, a1, a2, a3), (x0, x1, x2, x3))

    @pl.when(s == 1)
    def _():
        join((x0, x1, x2, x3), (here, d1, d2, d3))

    vt1[...] = flip(first[2])
    kt2[...] = flip(second[1])
    kt1[...] = flip(first[1])

    def softmax(keys, q, i):
        st = score_block(keys, q, i)
        top = jnp.max(st, axis=0, keepdims=True)
        p = jnp.exp2(st - top)
        return p * (1.0 / jnp.sum(p, axis=0, keepdims=True))

    def forward(i):
        n = (i + 1) * BLK
        cols = slice(i * BLK, n)
        p = softmax(first.at[1], first.at[0], i)
        p1[0:n, cols] = p
        out = dot(vt1[:, 0:n], p.astype(BF)).astype(BF)
        ot1[:, cols] = out
        second[0, cols] = (second[0, cols].astype(F32) + out.astype(F32).T).astype(BF)

    def both(i):
        n = (i + 1) * BLK
        cols = slice(i * BLK, n)
        dp = dot_nt(second[2, 0:n], second[3, cols])
        st = score_block(second.at[1], second.at[0], i)
        top = jnp.max(st, axis=0, keepdims=True)
        p = jnp.exp2(st - top)
        share = 1.0 / jnp.sum(p, axis=0, keepdims=True)
        delta = jnp.sum(p * dp, axis=0, keepdims=True) * share
        p = p * share
        backward_block(i, p, dp, delta, kt2, second.at[0], second.at[3], g1, dk2, dv2)
        dq2[cols] = flip(g1[:, cols])

    def backward(i):
        n = (i + 1) * BLK
        cols = slice(i * BLK, n)
        delta = jnp.sum(g1[:, cols].astype(F32) * ot1[:, cols].astype(F32), axis=0, keepdims=True)
        dp = dot_nt(first[2, 0:n], dq2[cols])
        backward_block(i, p1[0:n, cols], dp, delta, kt1, first.at[0], dq2, dqt1, dk1, dv1)
        dq1[cols] = flip(dqt1[:, cols])

    for i in range(4):
        forward(i)
    for i in range(4):
        both(i)
    for i in range(4):
        backward(i)

    def block(b, part):
        return pl.ds(pl.multiple_of(b * BLK + part * HD, HD), HD)

    for b in range(4):
        rows = slice(b * HD, (b + 1) * HD)
        for out, part in ((keep, h), (give, 1 - h)):
            out[0, rows] = dq2[block(b, part)]
            out[1, rows] = (dk2[block(b, part)] * SCALE).astype(BF)
            out[2, rows] = dv2[block(b, part)].astype(BF)

    for k, out in enumerate((out0, out1, out2, out3)):
        rows = rows_of(z ^ k, BLK)
        out[0] = dq1[rows]
        out[1] = (dk1[rows] * SCALE).astype(BF)
        out[2] = dv1[rows].astype(BF)


def weave_kernel(info, keep, came, d0, d1, d2, d3, x3, x0, x1, c1, x2, c3, c2, here):
    z, h, s = info[0], info[1], info[2]
    row = lax.broadcasted_iota(jnp.int32, (256, 256), 0)
    col = lax.broadcasted_iota(jnp.int32, (256, 256), 1)
    wanted = jnp.where(col < HD, 2 * col + h, 2 * (col - HD) + 1 - h)
    put = jnp.where(row == wanted, 1.0, 0.0).astype(BF)

    def weave(out, k):
        rows = rows_of(z ^ k, HD)
        parts = [jnp.concatenate([x[j, rows, :] for j in range(3)], axis=1) for x in (keep, came)]
        woven = dot(put, jnp.concatenate(parts, axis=0)).astype(BF)
        for j in range(3):
            out[j] = woven[:, j * HD : (j + 1) * HD]

    @pl.when(s == 0)
    def _():
        here[...] = d0[...]
        for k, out in enumerate((x0, x1, x2, x3)):
            weave(out, k)

    @pl.when(s == 1)
    def _():
        for rows, out in ((d0, x0), (d1, x1), (d2, x2), (d3, x3)):
            out[...] = rows[...]
        for k, out in enumerate((here, c1, c2, c3)):
            weave(out, k)


def finish_kernel(info, *refs):
    a2, a3, a1, x3, x0, x1, c1, x2, c2, c3, here, out_hbm, out, sems = refs
    z, s = info[0], info[2]

    def place(slot_a, slot_b):
        for j in range(3):
            for k in range(4):
                out[j, :, head_cols(first_head(z ^ k))] = slot_a[k][j]

                @pl.when(is_inner(z ^ k))
                def _(k=k):
                    out[j, :, head_cols(second_head(z ^ k))] = slot_b[k][j]

            pltpu.make_async_copy(out.at[j], out_hbm.at[j], sems.at[j]).start()

    @pl.when(s == 0)
    def _():
        place((here, a1, a2, a3), (x0, x1, x2, x3))

    @pl.when(s == 1)
    def _():
        place((x0, x1, x2, x3), (here, c1, c2, c3))

    for j in range(3):
        pltpu.make_async_copy(out.at[j], out_hbm.at[j], sems.at[j]).wait()


def build(n_dp, n_tensor):
    def index(s, d, t):
        return (s * n_dp + d) * n_tensor + t

    def everywhere(rule):
        pairs = []
        for d in range(n_dp):
            for t in range(n_tensor):
                pairs += rule(d, t)
        return pairs

    def send(value, pairs):
        return lax.ppermute(value, AXES, pairs)

    def inward(src, slot, k):
        return everywhere(
            lambda d, t: [(index(src, d, t), index(slot, d ^ k, t))]
            if slot == 0 or (d ^ k) % 4 in (1, 2)
            else []
        )

    def outward(dst, slot, k):
        return [(b, a) for a, b in inward(dst, slot, k)]

    def swap_lines(value, cores):
        return send(
            value,
            everywhere(
                lambda d, t: [
                    (index(c, d, t), index(c, d, t ^ 1))
                    for c in cores
                    if c == 1 and len(cores) == 1 or c == 0 or d % 4 in (1, 2)
                ]
            ),
        )

    def body(projections, out_grad):
        s = lax.axis_index("section")
        z = lax.axis_index("dp") % 4
        h = lax.axis_index("tensor") % 2
        info = jnp.stack([z, h, s]).astype(jnp.int32)
        local = projections[0]
        rows, cols = local.shape[1:]
        half = ((4, rows // 2, cols), BF)
        chunk_in = ((CHUNK, HD), BF)
        chunk = ((3, BLK, HD), BF)
        vm = pltpu.VMEM
        tall, wide = vm((LEN, HD), BF), vm((HD, LEN), BF)
        acc = vm((LEN, HD), F32)

        inputs = [info] + [
            pltpu.with_memory_space_constraint(x, pltpu.HBM) for x in (local, out_grad)
        ]
        hbm = pl.BlockSpec(memory_space=pltpu.HBM)
        staging = [vm((4, rows, cols), BF), pltpu.SemaphoreType.DMA((4,)), vm((HD, cols), BF)]
        away, a2, a3, a1, near = call(
            pick_far_kernel,
            [half] + [chunk_in] * 3 + [((5 * CHUNK, HD), BF)],
            inputs,
            staging,
            spec=hbm,
        )
        came = swap_lines(away, (1,))
        a3 = send(a3, inward(0, 0, 3))
        a2 = send(a2, inward(0, 0, 2))
        a1 = send(a1, inward(0, 0, 1))
        (stash,) = call(
            pick_own_kernel, [((18 * HD, HD), BF)], inputs[:2], staging[:2], spec=hbm
        )
        x0, x1, x2, x3, here, d1, d2, d3 = call(
            pick_second_kernel, [chunk_in] * 8, [info, near, stash, came]
        )
        x3 = send(x3, inward(0, 1, 3) + inward(1, 0, 3))
        x0 = send(x0, inward(0, 1, 0) + inward(1, 0, 0))
        x1 = send(x1, inward(0, 1, 1) + inward(1, 0, 1))
        d1 = send(d1, inward(1, 1, 1))
        x2 = send(x2, inward(0, 1, 2) + inward(1, 0, 2))
        d3 = send(d3, inward(1, 1, 3))
        d2 = send(d2, inward(1, 1, 2))
        keep, give, d0, d1, d2, d3 = call(
            main_kernel,
            [((3, 4 * HD, HD), BF)] * 2 + [chunk] * 4,
            [info, a2, a3, a1, x3, x0, x1, d1, x2, d2, d3, here],
            [vm((3, LEN, HD), BF), vm((4, LEN, HD), BF)]
            + [wide] * 6
            + [vm((LEN, LEN), F32), tall, tall, acc, acc, acc, acc],
        )
        came = swap_lines(give, (0, 1))
        a3 = send(d3, outward(0, 0, 3))
        a2 = send(d2, outward(0, 0, 2))
        a1 = send(d1, outward(0, 0, 1))
        x3, x0, x1, c1, x2, c3, c2, here = call(
            weave_kernel, [chunk] * 8, [info, keep, came, d0, d1, d2, d3]
        )
        x3 = send(x3, outward(0, 1, 3) + outward(1, 0, 3))
        x0 = send(x0, outward(0, 1, 0) + outward(1, 0, 0))
        x1 = send(x1, outward(0, 1, 1) + outward(1, 0, 1))
        c1 = send(c1, outward(1, 1, 1))
        x2 = send(x2, outward(0, 1, 2) + outward(1, 0, 2))
        c3 = send(c3, outward(1, 1, 3))
        c2 = send(c2, outward(1, 1, 2))
        (out,) = call(
            finish_kernel,
            [((3, rows, cols), BF)],
            [info, a2, a3, a1, x3, x0, x1, c1, x2, c2, c3, here],
            [vm((3, rows, cols), BF), pltpu.SemaphoreType.DMA((3,))],
            out_spec=hbm,
        )
        return out[None]

    return body


def solution(mesh):
    body = build(mesh.shape["dp"], mesh.shape["tensor"])
    in_specs = (P("section", None, "dp", "tensor"), P("dp", "tensor"))
    out_specs = P("section", None, "dp", "tensor")
    return jax.shard_map(body, mesh=mesh, in_specs=in_specs, out_specs=out_specs, check_vma=False)
```
